32 devices in a mesh: blk: 16 (over z, y, x), scale: 2 (over core).
Axes of the slice: x: 2, y: 2, z: 4, core: 2. Of those that a mesh axis runs over, the one named last changes fastest.
Arguments:
- start_block: float32 [64, 32768], P(None, ('blk', 'scale')), may hold values from -90 to 90
- blocks: bfloat16 [1024, 128, 128], P(('blk', 'scale')), may hold values from -0.1875 to 0.1875
- block_column: int32 [1024], P(('blk', 'scale')), may hold values from 0 to 7
- block_target: int32 [1024], P(('blk', 'scale')), may hold values from 0 to 15, as said below
- block_count: int32 [32], P(('blk', 'scale')), may hold values from 2 to 32, as said below
- partner: int32 [32768], P(('blk', 'scale')), may hold values from 0 to 1023, as said below
- degree: int32 [32768], P(('blk', 'scale')), may hold values from 1 to 16
Outputs:
- subspace: float32 [64, 32768], P(None, ('blk', 'scale'))
- rayleigh: float32 [64, 64], replicated
The draws below stay inside these ranges and needn't reach their ends.
Inputs may be any that keep to these rules, and one draw needn't show every extreme that they name: block_count[g] is the number of live slots of row group g; it is at least 2; some row group has all 32 slots live in every draw. In each row group, slots c < 2 have block_target of 8 or more, and all other slots have block_target below 8. Within each row group, partner is a permutation of 0 to 1023, and the pairing is mutual: if node i of group (b, s) has partner j, then node j of group (b, s xor 1) has partner i.
All inputs are finite; a program needn't handle non-finite values.
Results may differ from the reference program's by a relative error of at most 0.0011.
Values may be sent and summed in bfloat16 or wider, within the bound.
A program may use at most 64 MiB of HBM per device.

```python
import jax
import jax.numpy as jnp
from jax import lax

K = 64
BLOCK = 128
R_DEV = 1024
CAP = 32
ITERS = 2
RB = 8
CROSS = 2
TILE_GROUPS = 16
SCALE_GROUPS = 2
NODES = 32768
SLOTS = 1024


def draw_start_block(key, part):
    key_base, key_cols, key_rows = jax.random.split(jax.random.fold_in(key, 11), 3)
    position = jnp.arange(NODES).astype(jnp.float32) / NODES
    col_scale = 10.0 ** (jax.random.uniform(key_cols, (1, NODES), jnp.float32) - 0.5)
    row_scale = 10.0 ** (jax.random.uniform(key_rows, (K, 1), jnp.float32) - 0.5)
    base = jax.random.truncated_normal(key_base, -4.0, 4.0, (K, NODES), jnp.float32)
    ramp = (1.0 + 2.0 * position) / 2.0
    return (base * row_scale * col_scale * ramp[None, :]).astype(jnp.float32)


def draw_block_target(key, part):
    groups = TILE_GROUPS * SCALE_GROUPS
    key_near, key_far = jax.random.split(jax.random.fold_in(key, 47), 2)
    near = jax.random.randint(key_near, (groups, CAP), 0, RB)
    far = jax.random.randint(key_far, (groups, CAP), RB, 2 * RB)
    slot_index = jnp.arange(CAP, dtype=jnp.int32)[None, :]
    return jnp.where(slot_index < CROSS, far, near).reshape(SLOTS).astype(jnp.int32)


def draw_block_count(key, part):
    groups = TILE_GROUPS * SCALE_GROUPS
    key_first, key_second, key_full = jax.random.split(jax.random.fold_in(key, 23), 3)
    first = jax.random.randint(key_first, (groups,), CROSS, CAP + 1)
    second = jax.random.randint(key_second, (groups,), CROSS, CAP + 1)
    fullest = jax.random.randint(key_full, (), 0, groups)
    return jnp.minimum(first, second).at[fullest].set(CAP).astype(jnp.int32)


def draw_partner(key, part):
    pairs = SCALE_GROUPS // 2
    scores = jax.random.randint(jax.random.fold_in(key, 37), (TILE_GROUPS, pairs, R_DEV), 0, 2 ** 19)
    scores = scores * R_DEV + jnp.arange(R_DEV, dtype=jnp.int32)[None, None, :]
    forward_map = jnp.argsort(scores, axis=-1).astype(jnp.int32)
    inverse_map = jnp.argsort(forward_map, axis=-1).astype(jnp.int32)
    joined = jnp.stack([forward_map, inverse_map], axis=2)
    return joined.reshape(NODES).astype(jnp.int32)


def set_ends(drawn, stream_key, low, high):
    dims = drawn.shape
    place = [jax.random.randint(jax.random.fold_in(stream_key, axis), (), 0, dims[axis]) for axis in range(len(dims))]
    drawn = drawn.at[tuple(place)].set(low)
    longest = dims.index(max(dims))
    place[longest] = (place[longest] + 1) % dims[longest]
    return drawn.at[tuple(place)].set(high)


def steps_of(key, extent, cuts, least, largest):
    gain, own = 1.0, jax.random.fold_in(key, 6)
    for dim, blocks in cuts:
        draws = jnp.exp(jax.random.uniform(jax.random.fold_in(own, dim), (blocks,), jnp.float32, least / len(cuts), largest / len(cuts)))
        gain = gain * jnp.repeat(draws, extent[dim] // blocks).reshape([-1 if axis == dim else 1 for axis in range(len(extent))])
    return gain


def bell_draw(key, extent, spread, most, pieces=(), kind=jnp.bfloat16):
    level = steps_of(key, extent, pieces, -0.22, 0.18) if pieces else 1.0
    entries = jax.random.normal(key, extent, jnp.float32) * spread * level
    return jnp.minimum(jnp.maximum(entries, -most), most).astype(kind)


def setup_inputs(seed: int = 0) -> dict:
    seeds = jax.random.split(jax.random.key(seed), 8)
    return {
        "start_block": draw_start_block(jax.random.fold_in(seeds[7], 71), 0),
        "blocks": bell_draw(seeds[1], (SLOTS, BLOCK, BLOCK), 1024 ** -0.5, 0.1875, ((0, 32),)),
        "block_column": set_ends(jax.random.randint(seeds[2], (SLOTS,), 0, RB), jax.random.fold_in(seeds[2], 1), 0, RB - 1).astype(jnp.int32),
        "block_target": draw_block_target(jax.random.fold_in(seeds[7], 71), 0),
        "block_count": draw_block_count(jax.random.fold_in(seeds[7], 71), 0),
        "partner": draw_partner(jax.random.fold_in(seeds[7], 71), 0),
        "degree": set_ends(jax.random.randint(seeds[6], (NODES,), 1, 17), jax.random.fold_in(seeds[6], 1), 1, 16).astype(jnp.int32),
    }


FULL_PRECISION = lax.Precision.HIGHEST

def cycle_terms(packed):
    own_vectors, next_vectors, weights, columns, targets, counts = packed
    row_blocks = R_DEV // 128
    live_mask = (jnp.arange(CAP)[None, :] < counts[:, None]).astype(jnp.float32)
    onecol = (columns[:, :, None] == jnp.arange(row_blocks)[None, None, :]).astype(jnp.float32) * live_mask[:, :, None]
    onetgt = (targets[:, :, None] == jnp.arange(2 * row_blocks)[None, None, :]).astype(jnp.float32) * live_mask[:, :, None]
    stacked = jnp.concatenate([own_vectors, next_vectors], axis=2).astype(jnp.float32)
    picked_cols = jnp.einsum('scr,skrj->sckj', onecol, own_vectors.astype(jnp.float32), precision=FULL_PRECISION)
    picked_tgts = jnp.einsum('sct,sktj->sckj', onetgt, stacked, precision=FULL_PRECISION)
    weights = weights.astype(jnp.float32)
    forward = jnp.einsum('scki,scji->sckj', picked_cols, weights, precision=FULL_PRECISION)
    backward = jnp.einsum('sckj,scji->scki', picked_tgts, weights, precision=FULL_PRECISION)
    nearby = jnp.einsum('scr,sckj->skrj', onetgt[:, :, :row_blocks], forward, precision=FULL_PRECISION)
    nearby = nearby + jnp.einsum('scr,sckj->skrj', onecol, backward, precision=FULL_PRECISION)
    ahead_sum = jnp.einsum('scr,sckj->skrj', onetgt[:, :, row_blocks:], forward, precision=FULL_PRECISION)
    return (nearby, ahead_sum)

def apply_operator(vectors, inv_sqrt_degree, blocks, block_column, block_target, block_count, partner):
    row_blocks = R_DEV // 128
    scaled = (vectors * inv_sqrt_degree[None, :]).astype(jnp.bfloat16)
    arranged = scaled.reshape(K, TILE_GROUPS, SCALE_GROUPS, row_blocks, 128).transpose(1, 2, 0, 3, 4)
    following = jnp.roll(arranged, -1, axis=0)
    packed = (arranged, following, blocks.reshape(TILE_GROUPS, SCALE_GROUPS, CAP, 128, 128), block_column.reshape(TILE_GROUPS, SCALE_GROUPS, CAP), block_target.reshape(TILE_GROUPS, SCALE_GROUPS, CAP), block_count.reshape(TILE_GROUPS, SCALE_GROUPS))
    nearby, ahead_sum = lax.map(cycle_terms, packed)
    surface = nearby + jnp.roll(ahead_sum, 1, axis=0)
    surface = surface.transpose(2, 0, 1, 3, 4).reshape(K, NODES)
    paired = scaled.reshape(K, TILE_GROUPS, SCALE_GROUPS // 2, 2, R_DEV)[:, :, :, ::-1, :]
    indices = jnp.broadcast_to(partner.reshape(1, TILE_GROUPS, SCALE_GROUPS // 2, 2, R_DEV), paired.shape)
    crossed = jnp.take_along_axis(paired, indices, axis=4).reshape(K, NODES).astype(jnp.float32)
    return vectors + inv_sqrt_degree[None, :] * (surface + crossed)

def orthonormal(images):
    gram_matrix = jnp.dot(images, images.T, precision=FULL_PRECISION) / NODES
    factor = jnp.linalg.cholesky(gram_matrix)
    factor_inverse = jax.scipy.linalg.solve_triangular(factor, jnp.eye(K, dtype=jnp.float32), lower=True)
    return jnp.dot(factor_inverse, images, precision=FULL_PRECISION)

def reference(start_block, blocks, block_column, block_target, block_count, partner, degree):
    inv_sqrt_degree = 1.0 / jnp.sqrt(degree.astype(jnp.float32))
    subspace = start_block
    for sweep_index in range(ITERS):
        subspace = orthonormal(apply_operator(subspace, inv_sqrt_degree, blocks, block_column, block_target, block_count, partner))
    images = apply_operator(subspace, inv_sqrt_degree, blocks, block_column, block_target, block_count, partner)
    rayleigh = jnp.dot(subspace, images.T, precision=FULL_PRECISION) / NODES
    return (subspace, rayleigh)
```

```python
import functools

import jax
import jax.numpy as jnp
from jax import lax
from jax.experimental import pallas as pl
from jax.experimental.pallas import tpu as pltpu
from jax.sharding import PartitionSpec as P

ITERS = 2
BLOCK = 128
CROSS = 2
PANEL = 8
MESH = pl.DeviceIdType.MESH
FULL = lax.Precision.HIGHEST


def group_stages(total):
    stages, stride = [], 1
    while stride < total:
        size = min(8, total // stride)
        stages.append((stride, size))
        stride *= size
    return stages


def prepare(
    column_ref, target_ref, count_ref, blocks_ref, partner_ref,
    high_ref, low_ref, pair_ref, back_ref, turned_ref, aim_ref, dense,
):
    nodes = dense.shape[0]
    dense[...] = jnp.zeros_like(dense)
    back_ref[...] = jnp.zeros_like(back_ref)

    def spot(index):
        return pl.ds(pl.multiple_of(index * BLOCK, BLOCK), BLOCK)

    for slot in range(CROSS):
        weight = blocks_ref[slot]
        rows = pl.ds(slot * BLOCK, BLOCK)
        back_ref[rows, spot(column_ref[slot])] = weight
        turned_ref[rows, :] = weight.astype(jnp.float32).T.astype(jnp.bfloat16)
        aim_ref[slot, 0] = jnp.full((8, BLOCK), target_ref[slot] - nodes // BLOCK, jnp.int32)
        aim_ref[slot, 1] = jnp.full((8, BLOCK), column_ref[slot], jnp.int32)

    def place(slot, carry):
        weight = blocks_ref[slot].astype(jnp.float32)
        rows, columns = spot(target_ref[slot]), spot(column_ref[slot])
        dense[rows, columns] += weight
        dense[columns, rows] += weight.T
        return carry

    lax.fori_loop(CROSS, count_ref[0], place, 0)
    high = dense[...].astype(jnp.bfloat16)
    high_ref[...] = high
    low_ref[...] = (dense[...] - high.astype(jnp.float32)).astype(jnp.bfloat16)
    index = lax.broadcasted_iota(jnp.int32, (nodes, nodes), 0)
    pair_ref[...] = (index == partner_ref[...]).astype(jnp.float32).astype(jnp.bfloat16)


def inverse_factor(gram):
    size = gram.shape[0]
    rows = lax.broadcasted_iota(jnp.int32, (size, size), 0)
    columns = lax.broadcasted_iota(jnp.int32, (size, size), 1)
    whole = jnp.concatenate([gram, (rows == columns).astype(jnp.float32)], axis=1)
    width = 2 * size
    place = lax.broadcasted_iota(jnp.int32, (size, width), 0)

    def eliminate(panel, whole):
        active = place < size - PANEL * panel
        strips = [jnp.broadcast_to(whole[:, k : k + 1], (size, width)) for k in range(PANEL)]
        pivots = []
        for j in range(PANEL):
            pivot = strips[j][j : j + 1, :]
            pivots.append(pivot)
            factor = jnp.where(active & (place > j), strips[j] * (1.0 / pivot), 0.0)
            for k in range(j + 1, PANEL):
                strips[k] = strips[k] - factor * strips[k][j : j + 1, :]
            whole = whole - factor * whole[j : j + 1, :]
        done = whole[:PANEL] * (1.0 / jnp.sqrt(jnp.concatenate(pivots, axis=0)))
        whole = jnp.concatenate([whole[PANEL:], done], axis=0)
        return pltpu.roll(whole, width - PANEL, 1)

    return lax.fori_loop(0, size // PANEL, eliminate, whole)[:, :size]


def iterate(
    blk_total, scale_total,
    start_ref, degree_ref, high_ref, low_ref, pair_ref, back_ref, turned_ref, aim_ref,
    subspace_ref, rayleigh_ref,
    scaled_buf, partner_buf, ahead_out, behind_out, ahead_in, behind_in,
    turned_in, aim_in, forward_weights, *rest,
):
    stages = group_stages(blk_total * scale_total)
    gather_bufs = rest[: len(stages)]
    pair_send, pair_recv, edge_send, edge_recv, gather_send, gather_recv = rest[len(stages):]
    vectors, nodes = start_ref.shape
    row_blocks = nodes // BLOCK
    node_total = nodes * blk_total * scale_total
    blk, scale = lax.axis_index("blk"), lax.axis_index("scale")
    me = blk * scale_total + scale
    ahead = ((blk + 1) % blk_total, scale)
    behind = ((blk + blk_total - 1) % blk_total, scale)
    partner = (blk, scale + 1 - 2 * (scale % 2))

    def peer(stride, size, shift):
        digit = (me // stride) % size
        other = (digit + shift) % size
        place = me + (other - digit) * stride
        return other, (place // scale_total, place % scale_total)

    barrier = pltpu.get_barrier_semaphore()
    greeted = [ahead, behind]
    for stride, size in stages:
        greeted += [peer(stride, size, shift)[1] for shift in range(1, size)]
    for device in greeted:
        pl.semaphore_signal(barrier, inc=1, device_id=device, device_id_type=MESH)

    inv_sqrt_degree = 1.0 / jnp.sqrt(degree_ref[...].astype(jnp.float32))
    sent = []

    def send(source, target, send_sem, recv_sem, device):
        copy = pltpu.make_async_remote_copy(
            src_ref=source, dst_ref=target, send_sem=send_sem, recv_sem=recv_sem,
            device_id=device, device_id_type=MESH,
        )
        copy.start()
        sent.append(copy)
        return copy

    def chosen(values, marks):
        picked = jnp.zeros((vectors, BLOCK), jnp.float32)
        mark = jnp.broadcast_to(marks[:1, :], (vectors, BLOCK))
        for r in range(row_blocks):
            picked = jnp.where(mark == r, values[:, r * BLOCK : (r + 1) * BLOCK], picked)
        return picked.astype(jnp.bfloat16)

    def product(left, right):
        return jnp.dot(left, right, preferred_element_type=jnp.float32)

    def operate(step, current):
        scaled = (current * inv_sqrt_degree).astype(jnp.bfloat16)
        scaled_buf[step] = scaled
        if step == 0:
            pl.semaphore_wait(barrier, len(greeted))
            weights_copy = send(turned_ref, turned_in, edge_send.at[6], edge_recv.at[6], ahead)
            aim_copy = send(aim_ref, aim_in, edge_send.at[7], edge_recv.at[7], ahead)
        pair_copy = send(
            scaled_buf.at[step], partner_buf.at[step], pair_send.at[step], pair_recv.at[step], partner
        )
        wide = scaled.astype(jnp.float32)
        for slot in range(CROSS):
            ahead_out[step, :, slot * BLOCK : (slot + 1) * BLOCK] = chosen(wide, aim_ref[slot, 1])
        ahead_copy = send(
            ahead_out.at[step], behind_in.at[step], edge_send.at[2 * step], edge_recv.at[2 * step], ahead
        )
        if step == 0:
            weights_copy.wait_recv()
            aim_copy.wait_recv()
            for slot in range(CROSS):
                span = slice(slot * BLOCK, (slot + 1) * BLOCK)
                weight = turned_in[span, :].astype(jnp.float32)
                mark = jnp.broadcast_to(aim_in[slot, 0][:1, :], (BLOCK, BLOCK))
                for r in range(row_blocks):
                    forward_weights[span, r * BLOCK : (r + 1) * BLOCK] = jnp.where(
                        mark == r, weight, 0.0
                    ).astype(jnp.bfloat16)
        for slot in range(CROSS):
            behind_out[step, :, slot * BLOCK : (slot + 1) * BLOCK] = chosen(wide, aim_in[slot, 0])
        behind_copy = send(
            behind_out.at[step], ahead_in.at[step],
            edge_send.at[2 * step + 1], edge_recv.at[2 * step + 1], behind,
        )
        total = product(scaled, high_ref[...]) + product(scaled, low_ref[...])
        pair_copy.wait_recv()
        total += product(partner_buf[step], pair_ref[...])
        ahead_copy.wait_recv()
        total += product(behind_in[step], forward_weights[...])
        behind_copy.wait_recv()
        total += product(ahead_in[step], back_ref[...])
        return current + inv_sqrt_degree * total

    def over_devices(step, local):
        half = vectors // 2
        value = jnp.concatenate([local[:half], local[half:]], axis=1)
        slot_base = 0
        for (stride, size), buf in zip(stages, gather_bufs):
            digit = (me // stride) % size
            buf[step, digit] = value
            copies = []
            for shift in range(1, size):
                other, device = peer(stride, size, shift)
                copies.append(send(
                    buf.at[step, digit], buf.at[step, digit],
                    gather_send.at[step, slot_base + shift], gather_recv.at[step, slot_base + digit],
                    device,
                ))
            for shift in range(1, size):
                other, device = peer(stride, size, shift)
                pltpu.make_async_remote_copy(
                    src_ref=buf.at[step, digit], dst_ref=buf.at[step, other],
                    send_sem=gather_send.at[step, slot_base + shift],
                    recv_sem=gather_recv.at[step, slot_base + other],
                    device_id=device, device_id_type=MESH,
                ).wait_recv()
            value = buf[step, 0]
            for other in range(1, size):
                value = value + buf[step, other]
            slot_base += size
        return jnp.concatenate([value[:, :vectors], value[:, vectors:]], axis=0) / node_total

    def inner(left, right):
        return lax.dot_general(
            left, right, (((1,), (1,)), ((), ())), precision=FULL, preferred_element_type=jnp.float32
        )

    subspace = start_ref[...]
    for step in range(ITERS):
        images = operate(step, subspace)
        gram = over_devices(step, inner(images, images))
        subspace = jnp.dot(
            inverse_factor(gram), images, precision=FULL, preferred_element_type=jnp.float32
        )
    subspace_ref[...] = subspace
    images = operate(ITERS, subspace)
    rayleigh_ref[...] = over_devices(ITERS, inner(subspace, images))
    for copy in sent:
        copy.wait_send()


def solution(mesh):
    blk_total, scale_total = mesh.shape["blk"], mesh.shape["scale"]
    stages = group_stages(blk_total * scale_total)

    def shards(start_block, blocks, block_column, block_target, block_count, partner, degree):
        vectors, nodes = start_block.shape
        vmem = pl.BlockSpec(memory_space=pltpu.VMEM)
        smem = pl.BlockSpec(memory_space=pltpu.SMEM)
        half = jnp.bfloat16
        prepared = pl.pallas_call(
            prepare,
            out_shape=(
                jax.ShapeDtypeStruct((nodes, nodes), half),
                jax.ShapeDtypeStruct((nodes, nodes), half),
                jax.ShapeDtypeStruct((nodes, nodes), half),
                jax.ShapeDtypeStruct((CROSS * BLOCK, nodes), half),
                jax.ShapeDtypeStruct((CROSS * BLOCK, BLOCK), half),
                jax.ShapeDtypeStruct((CROSS, 2, 8, BLOCK), jnp.int32),
            ),
            in_specs=[smem, smem, smem, vmem, vmem],
            out_specs=(vmem,) * 6,
            scratch_shapes=[pltpu.VMEM((nodes, nodes), jnp.float32)],
            compiler_params=pltpu.CompilerParams(vmem_limit_bytes=32 * 2**20),
        )(block_column, block_target, block_count, blocks, partner.reshape(1, nodes))
        steps = ITERS + 1
        edge = pltpu.VMEM((steps, vectors, CROSS * BLOCK), half)
        counts = sum(size for _, size in stages)
        return pl.pallas_call(
            functools.partial(iterate, blk_total, scale_total),
            out_shape=(
                jax.ShapeDtypeStruct((vectors, nodes), jnp.float32),
                jax.ShapeDtypeStruct((vectors, vectors), jnp.float32),
            ),
            in_specs=[vmem] * 8,
            out_specs=(vmem, vmem),
            scratch_shapes=[
                pltpu.VMEM((steps, vectors, nodes), half),
                pltpu.VMEM((steps, vectors, nodes), half),
                edge, edge, edge, edge,
                pltpu.VMEM((CROSS * BLOCK, BLOCK), half),
                pltpu.VMEM((CROSS, 2, 8, BLOCK), jnp.int32),
                pltpu.VMEM((CROSS * BLOCK, nodes), half),
                *[
                    pltpu.VMEM((steps, size, vectors // 2, 2 * vectors), jnp.float32)
                    for _, size in stages
                ],
                pltpu.SemaphoreType.DMA((steps,)),
                pltpu.SemaphoreType.DMA((steps,)),
                pltpu.SemaphoreType.DMA((2 * steps + 2,)),
                pltpu.SemaphoreType.DMA((2 * steps + 2,)),
                pltpu.SemaphoreType.DMA((steps, counts)),
                pltpu.SemaphoreType.DMA((steps, counts)),
            ],
            compiler_params=pltpu.CompilerParams(
                collective_id=0, has_side_effects=True, vmem_limit_bytes=40 * 2**20
            ),
        )(start_block, degree.reshape(1, nodes), *prepared)

    return jax.shard_map(
        shards,
        mesh=mesh,
        in_specs=(
            P(None, ("blk", "scale")),
            P(("blk", "scale"), None, None),
            P(("blk", "scale")),
            P(("blk", "scale")),
            P(("blk", "scale")),
            P(("blk", "scale")),
            P(("blk", "scale")),
        ),
        out_specs=(P(None, ("blk", "scale")), P()),
        check_vma=False,
    )
```

```python
import functools

import jax
import jax.numpy as jnp
from jax import lax
from jax.experimental import pallas as pl
from jax.experimental.pallas import tpu as pltpu
from jax.sharding import PartitionSpec as P

STEPS = 3
BLOCK = 128
CROSS = 2
PANEL = 8
MESH = pl.DeviceIdType.MESH
FULL = lax.Precision.HIGHEST


def group_stages(total):
    stages, stride = [], 1
    while stride < total:
        size = min(8, total // stride)
        stages.append((stride, size))
        stride *= size
    return stages


def prepare(
    column_ref, target_ref, count_ref, blocks_ref, partner_ref,
    high_ref, low_ref, pair_ref, back_ref, turned_ref, aim_ref, dense,
):
    nodes = dense.shape[0]
    dense[...] = jnp.zeros_like(dense)
    back_ref[...] = jnp.zeros_like(back_ref)

    def spot(index):
        return pl.ds(pl.multiple_of(index * BLOCK, BLOCK), BLOCK)

    for slot in range(CROSS):
        weight = blocks_ref[slot]
        rows = pl.ds(slot * BLOCK, BLOCK)
        back_ref[rows, spot(column_ref[slot])] = weight
        turned_ref[rows, :] = weight.astype(jnp.float32).T.astype(jnp.bfloat16)
        aim_ref[slot, 0] = jnp.full((8, BLOCK), target_ref[slot] - nodes // BLOCK, jnp.int32)
        aim_ref[slot, 1] = jnp.full((8, BLOCK), column_ref[slot], jnp.int32)

    def place(slot, carry):
        weight = blocks_ref[slot].astype(jnp.float32)
        rows, columns = spot(target_ref[slot]), spot(column_ref[slot])
        dense[rows, columns] += weight
        dense[columns, rows] += weight.T
        return carry

    lax.fori_loop(CROSS, count_ref[0], place, 0)
    high = dense[...].astype(jnp.bfloat16)
    high_ref[...] = high
    low_ref[...] = (dense[...] - high.astype(jnp.float32)).astype(jnp.bfloat16)
    index = lax.broadcasted_iota(jnp.int32, (nodes, nodes), 0)
    pair_ref[...] = (index == partner_ref[...]).astype(jnp.float32).astype(jnp.bfloat16)


def inverse_factor(gram):
    size = gram.shape[0]
    rows = lax.broadcasted_iota(jnp.int32, (size, size), 0)
    columns = lax.broadcasted_iota(jnp.int32, (size, size), 1)
    whole = jnp.concatenate([gram, (rows == columns).astype(jnp.float32)], axis=1)
    width = 2 * size
    place = lax.broadcasted_iota(jnp.int32, (size, width), 0)

    def eliminate(panel, whole):
        active = place < size - PANEL * panel
        strips = [jnp.broadcast_to(whole[:, k : k + 1], (size, width)) for k in range(PANEL)]
        pivots = []
        for j in range(PANEL):
            pivot = strips[j][j : j + 1, :]
            pivots.append(pivot)
            factor = jnp.where(active & (place > j), strips[j] * (1.0 / pivot), 0.0)
            for k in range(j + 1, PANEL):
                strips[k] = strips[k] - factor * strips[k][j : j + 1, :]
            whole = whole - factor * whole[j : j + 1, :]
        done = whole[:PANEL] * (1.0 / jnp.sqrt(jnp.concatenate(pivots, axis=0)))
        whole = jnp.concatenate([whole[PANEL:], done], axis=0)
        return pltpu.roll(whole, width - PANEL, 1)

    return lax.fori_loop(0, size // PANEL, eliminate, whole)[:, :size]


def iterate(
    blk_total, scale_total,
    start_ref, degree_ref, high_ref, low_ref, pair_ref, back_ref, turned_ref, aim_ref,
    subspace_ref, rayleigh_ref,
    scaled_buf, partner_buf, ahead_out, behind_out, ahead_in, behind_in,
    turned_in, aim_in, forward_weights, *rest,
):
    stages = group_stages(blk_total * scale_total)
    gather_bufs = rest[: len(stages)]
    pair_send, pair_recv, edge_send, edge_recv, gather_send, gather_recv = rest[len(stages):]
    vectors, nodes = start_ref.shape
    row_blocks = nodes // BLOCK
    node_total = nodes * blk_total * scale_total
    blk, scale = lax.axis_index("blk"), lax.axis_index("scale")
    me = blk * scale_total + scale
    ahead = ((blk + 1) % blk_total, scale)
    behind = ((blk + blk_total - 1) % blk_total, scale)
    partner = (blk, scale + 1 - 2 * (scale % 2))

    def peer(stride, size, shift):
        digit = (me // stride) % size
        other = (digit + shift) % size
        place = me + (other - digit) * stride
        return other, (place // scale_total, place % scale_total)

    barrier = pltpu.get_barrier_semaphore()
    greeted = [ahead, behind]
    for stride, size in stages:
        greeted += [peer(stride, size, shift)[1] for shift in range(1, size)]
    for device in greeted:
        pl.semaphore_signal(barrier, inc=1, device_id=device, device_id_type=MESH)

    inv_sqrt_degree = 1.0 / jnp.sqrt(degree_ref[...].astype(jnp.float32))
    sent = []

    def send(source, target, send_sem, recv_sem, device):
        copy = pltpu.make_async_remote_copy(
            src_ref=source, dst_ref=target, send_sem=send_sem, recv_sem=recv_sem,
            device_id=device, device_id_type=MESH,
        )
        copy.start()
        sent.append(copy)
        return copy

    def chosen(values, marks):
        height = values.shape[0]
        picked = jnp.zeros((height, BLOCK), jnp.float32)
        mark = jnp.broadcast_to(marks[:1, :], (height, BLOCK))
        for r in range(row_blocks):
            picked = jnp.where(mark == r, values[:, r * BLOCK : (r + 1) * BLOCK], picked)
        return picked.astype(jnp.bfloat16)

    def product(left, right):
        return jnp.dot(left, right, preferred_element_type=jnp.float32)

    def depart(step, current):
        exact = current * inv_sqrt_degree
        scaled = exact.astype(jnp.bfloat16)
        wide = scaled.astype(jnp.float32)
        if step > 0:
            wide = jnp.concatenate([wide, exact - wide], axis=0)
            scaled = wide.astype(jnp.bfloat16)
        height = wide.shape[0]
        rows = pl.ds(0, height)
        scaled_buf[step, :height] = scaled
        for slot in range(CROSS):
            span = slice(slot * BLOCK, (slot + 1) * BLOCK)
            ahead_out[step, :height, span] = chosen(wide, aim_ref[slot, 1])
        if step == 0:
            pl.semaphore_wait(barrier, len(greeted))
            weights_copy = send(turned_ref, turned_in, edge_send.at[6], edge_recv.at[6], ahead)
            aim_copy = send(aim_ref, aim_in, edge_send.at[7], edge_recv.at[7], ahead)
        ahead_copy = send(
            ahead_out.at[step, rows], behind_in.at[step, rows],
            edge_send.at[2 * step], edge_recv.at[2 * step], ahead,
        )
        pair_copy = send(
            scaled_buf.at[step, rows], partner_buf.at[step, rows],
            pair_send.at[step], pair_recv.at[step], partner,
        )
        if step == 0:
            aim_copy.wait_recv()
        for slot in range(CROSS):
            span = slice(slot * BLOCK, (slot + 1) * BLOCK)
            behind_out[step, :height, span] = chosen(wide, aim_in[slot, 0])
        behind_copy = send(
            behind_out.at[step, rows], ahead_in.at[step, rows],
            edge_send.at[2 * step + 1], edge_recv.at[2 * step + 1], behind,
        )
        if step == 0:
            weights_copy.wait_recv()
            for slot in range(CROSS):
                span = slice(slot * BLOCK, (slot + 1) * BLOCK)
                weight = turned_in[span, :].astype(jnp.float32)
                mark = jnp.broadcast_to(aim_in[slot, 0][:1, :], (BLOCK, BLOCK))
                for r in range(row_blocks):
                    forward_weights[span, r * BLOCK : (r + 1) * BLOCK] = jnp.where(
                        mark == r, weight, 0.0
                    ).astype(jnp.bfloat16)
        return height, scaled, pair_copy, ahead_copy, behind_copy

    def nearby(trip):
        return product(trip[1], high_ref[...]) + product(trip[1], low_ref[...])

    def arrive(step, current, trip, total):
        height, _, pair_copy, ahead_copy, behind_copy = trip
        pair_copy.wait_recv()
        total += product(partner_buf[step, :height], pair_ref[...])
        ahead_copy.wait_recv()
        total += product(behind_in[step, :height], forward_weights[...])
        behind_copy.wait_recv()
        total += product(ahead_in[step, :height], back_ref[...])
        if height > vectors:
            total = total[:vectors] + total[vectors:]
        return current + inv_sqrt_degree * total

    bases = [sum(size for _, size in stages[:level]) for level in range(len(stages))]

    def share(which, level, value):
        (stride, size), buf, base = stages[level], gather_bufs[level], bases[level]
        digit = (me // stride) % size
        buf[which, digit] = value
        for shift in range(1, size):
            send(
                buf.at[which, digit], buf.at[which, digit],
                gather_send.at[which, base + shift], gather_recv.at[which, base + digit],
                peer(stride, size, shift)[1],
            )

    def collect(which, level):
        (stride, size), buf, base = stages[level], gather_bufs[level], bases[level]
        digit = (me // stride) % size
        for shift in range(1, size):
            other, device = peer(stride, size, shift)
            pltpu.make_async_remote_copy(
                src_ref=buf.at[which, digit], dst_ref=buf.at[which, other],
                send_sem=gather_send.at[which, base + shift],
                recv_sem=gather_recv.at[which, base + other],
                device_id=device, device_id_type=MESH,
            ).wait_recv()
        value = buf[which, 0]
        for other in range(1, size):
            value = value + buf[which, other]
        return value

    def advance(which, level):
        value = collect(which, level)
        if level + 1 < len(stages):
            share(which, level + 1, value)
        return value

    def folded(value):
        half = vectors // 2
        return jnp.concatenate([value[:half], value[half:]], axis=1)

    def unfolded(value):
        return jnp.concatenate([value[:, :vectors], value[:, vectors:]], axis=0) / node_total

    def inner(left, right):
        return lax.dot_general(
            left, right, (((1,), (1,)), ((), ())), precision=FULL, preferred_element_type=jnp.float32
        )

    def full(left, right):
        return jnp.dot(left, right, precision=FULL, preferred_element_type=jnp.float32)

    last = len(stages) - 1
    start = start_ref[...]
    trip = depart(0, start)
    first = arrive(0, start, trip, nearby(trip))
    trip = depart(1, first)
    share(0, 0, folded(inner(first, first)))
    total = nearby(trip)
    second = arrive(1, first, trip, total)
    trip = depart(2, second)
    advance(0, 0)
    share(1, 0, folded(inner(second, second)))
    total = nearby(trip)
    third = arrive(2, second, trip, total)
    share(2, 0, folded(inner(second, third)))
    for level in range(1, last):
        advance(0, level)
    advance(1, 0)
    first_inverse = inverse_factor(unfolded(collect(0, last)))
    for level in range(last):
        advance(2, level)
        if level + 1 < last:
            advance(1, level + 1)
    middle = inner(full(first_inverse, unfolded(collect(1, last))), first_inverse)
    change = full(inverse_factor(middle), first_inverse)
    subspace_ref[...] = full(change, second)
    rayleigh_ref[...] = inner(full(change, unfolded(collect(2, last))), change)
    for copy in sent:
        copy.wait_send()


def solution(mesh):
    blk_total, scale_total = mesh.shape["blk"], mesh.shape["scale"]
    stages = group_stages(blk_total * scale_total)

    def shards(start_block, blocks, block_column, block_target, block_count, partner, degree):
        vectors, nodes = start_block.shape
        vmem = pl.BlockSpec(memory_space=pltpu.VMEM)
        smem = pl.BlockSpec(memory_space=pltpu.SMEM)
        half = jnp.bfloat16
        prepared = pl.pallas_call(
            prepare,
            out_shape=(
                jax.ShapeDtypeStruct((nodes, nodes), half),
                jax.ShapeDtypeStruct((nodes, nodes), half),
                jax.ShapeDtypeStruct((nodes, nodes), half),
                jax.ShapeDtypeStruct((CROSS * BLOCK, nodes), half),
                jax.ShapeDtypeStruct((CROSS * BLOCK, BLOCK), half),
                jax.ShapeDtypeStruct((CROSS, 2, 8, BLOCK), jnp.int32),
            ),
            in_specs=[smem, smem, smem, vmem, vmem],
            out_specs=(vmem,) * 6,
            scratch_shapes=[pltpu.VMEM((nodes, nodes), jnp.float32)],
            compiler_params=pltpu.CompilerParams(vmem_limit_bytes=32 * 2**20),
        )(block_column, block_target, block_count, blocks, partner.reshape(1, nodes))
        steps = STEPS
        edge = pltpu.VMEM((steps, 2 * vectors, CROSS * BLOCK), half)
        counts = sum(size for _, size in stages)
        return pl.pallas_call(
            functools.partial(iterate, blk_total, scale_total),
            out_shape=(
                jax.ShapeDtypeStruct((vectors, nodes), jnp.float32),
                jax.ShapeDtypeStruct((vectors, vectors), jnp.float32),
            ),
            in_specs=[vmem] * 8,
            out_specs=(vmem, vmem),
            scratch_shapes=[
                pltpu.VMEM((steps, 2 * vectors, nodes), half),
                pltpu.VMEM((steps, 2 * vectors, nodes), half),
                edge, edge, edge, edge,
                pltpu.VMEM((CROSS * BLOCK, BLOCK), half),
                pltpu.VMEM((CROSS, 2, 8, BLOCK), jnp.int32),
                pltpu.VMEM((CROSS * BLOCK, nodes), half),
                *[
                    pltpu.VMEM((steps, size, vectors // 2, 2 * vectors), jnp.float32)
                    for _, size in stages
                ],
                pltpu.SemaphoreType.DMA((steps,)),
                pltpu.SemaphoreType.DMA((steps,)),
                pltpu.SemaphoreType.DMA((2 * steps + 2,)),
                pltpu.SemaphoreType.DMA((2 * steps + 2,)),
                pltpu.SemaphoreType.DMA((steps, counts)),
                pltpu.SemaphoreType.DMA((steps, counts)),
            ],
            compiler_params=pltpu.CompilerParams(
                collective_id=0, has_side_effects=True, vmem_limit_bytes=40 * 2**20
            ),
        )(start_block, degree.reshape(1, nodes), *prepared)

    return jax.shard_map(
        shards,
        mesh=mesh,
        in_specs=(
            P(None, ("blk", "scale")),
            P(("blk", "scale"), None, None),
            P(("blk", "scale")),
            P(("blk", "scale")),
            P(("blk", "scale")),
            P(("blk", "scale")),
            P(("blk", "scale")),
        ),
        out_specs=(P(None, ("blk", "scale")), P()),
        check_vma=False,
    )
```

```python
import functools

import jax
import jax.numpy as jnp
from jax import lax
from jax.experimental import pallas as pl
from jax.experimental.pallas import tpu as pltpu
from jax.sharding import PartitionSpec as P

STEPS = 3
BLOCK = 128
CROSS = 2
PANEL = 8
MESH = pl.DeviceIdType.MESH
FULL = lax.Precision.HIGHEST


def group_stages(total):
    stages, stride = [], 1
    while stride < total:
        size = min(8, total // stride)
        stages.append((stride, size))
        stride *= size
    return stages


def prepare(
    count_ref, column_src, target_src, blocks_src, partner_src, start_src, degree_src,
    dense, back_ref, turned_ref, aim_ref, partner_ref, start_ref, scale_ref,
    column_ref, target_ref, blocks_ref, degree_ref, arrived,
):
    nodes = dense.shape[0]
    pairs = (
        (column_src, column_ref), (target_src, target_ref), (blocks_src, blocks_ref),
        (partner_src, partner_ref), (start_src, start_ref), (degree_src, degree_ref),
    )
    copies = [
        pltpu.make_async_copy(source, target, arrived.at[k])
        for k, (source, target) in enumerate(pairs)
    ]
    for copy in copies:
        copy.start()
    dense[...] = jnp.zeros_like(dense)
    back_ref[...] = jnp.zeros_like(back_ref)
    for copy in copies:
        copy.wait()
    scale_ref[...] = 1.0 / jnp.sqrt(degree_ref[...].astype(jnp.float32))

    def spot(index):
        return pl.ds(pl.multiple_of(index * BLOCK, BLOCK), BLOCK)

    for slot in range(CROSS):
        weight = blocks_ref[slot]
        rows = pl.ds(slot * BLOCK, BLOCK)
        back_ref[rows, spot(column_ref[slot])] = weight
        turned_ref[rows, :] = weight.astype(jnp.float32).T.astype(jnp.bfloat16)
        aim_ref[slot, 0] = jnp.full((8, BLOCK), target_ref[slot] - nodes // BLOCK, jnp.int32)
        aim_ref[slot, 1] = jnp.full((8, BLOCK), column_ref[slot], jnp.int32)

    def place(slot, carry):
        weight = blocks_ref[slot].astype(jnp.float32)
        rows, columns = spot(target_ref[slot]), spot(column_ref[slot])
        dense[rows, columns] += weight
        dense[columns, rows] += weight.T
        return carry

    lax.fori_loop(CROSS, count_ref[0], place, 0)


def inverse_factor(gram):
    size = gram.shape[0]
    rows = lax.broadcasted_iota(jnp.int32, (size, size), 0)
    columns = lax.broadcasted_iota(jnp.int32, (size, size), 1)
    whole = jnp.concatenate([gram, (rows == columns).astype(jnp.float32)], axis=1)
    width = 2 * size
    place = lax.broadcasted_iota(jnp.int32, (size, width), 0)

    def eliminate(panel, whole):
        active = place < size - PANEL * panel
        strips = [jnp.broadcast_to(whole[:, k : k + 1], (size, width)) for k in range(PANEL)]
        pivots = []
        for j in range(PANEL):
            pivot = strips[j][j : j + 1, :]
            pivots.append(pivot)
            factor = jnp.where(active & (place > j), strips[j] * (1.0 / pivot), 0.0)
            for k in range(j + 1, PANEL):
                strips[k] = strips[k] - factor * strips[k][j : j + 1, :]
            whole = whole - factor * whole[j : j + 1, :]
        done = whole[:PANEL] * (1.0 / jnp.sqrt(jnp.concatenate(pivots, axis=0)))
        whole = jnp.concatenate([whole[PANEL:], done], axis=0)
        return pltpu.roll(whole, width - PANEL, 1)

    return lax.fori_loop(0, size // PANEL, eliminate, whole)[:, :size]


def iterate(
    blk_total, scale_total,
    dense_ref, back_ref, turned_ref, aim_ref, partner_ref, start_ref, scale_ref,
    subspace_ref, rayleigh_ref,
    scaled_buf, partner_buf, ahead_out, behind_out, ahead_in, behind_in,
    turned_in, aim_in, forward_weights, high_ref, low_ref, pair_ref, *rest,
):
    stages = group_stages(blk_total * scale_total)
    gather_bufs = rest[: len(stages)]
    pair_send, pair_recv, edge_send, edge_recv, gather_send, gather_recv = rest[len(stages):]
    vectors, nodes = start_ref.shape
    row_blocks = nodes // BLOCK
    node_total = nodes * blk_total * scale_total
    blk, scale = lax.axis_index("blk"), lax.axis_index("scale")
    me = blk * scale_total + scale
    ahead = ((blk + 1) % blk_total, scale)
    behind = ((blk + blk_total - 1) % blk_total, scale)
    partner = (blk, scale + 1 - 2 * (scale % 2))

    def peer(stride, size, shift):
        digit = (me // stride) % size
        other = (digit + shift) % size
        place = me + (other - digit) * stride
        return other, (place // scale_total, place % scale_total)

    barrier = pltpu.get_barrier_semaphore()
    greeted = [ahead, behind]
    for stride, size in stages:
        greeted += [peer(stride, size, shift)[1] for shift in range(1, size)]
    for device in greeted:
        pl.semaphore_signal(barrier, inc=1, device_id=device, device_id_type=MESH)

    inv_sqrt_degree = scale_ref[...]
    sent = []

    def send(source, target, send_sem, recv_sem, device):
        copy = pltpu.make_async_remote_copy(
            src_ref=source, dst_ref=target, send_sem=send_sem, recv_sem=recv_sem,
            device_id=device, device_id_type=MESH,
        )
        copy.start()
        sent.append(copy)
        return copy

    def chosen(values, marks):
        height = values.shape[0]
        picked = jnp.zeros((height, BLOCK), jnp.float32)
        mark = jnp.broadcast_to(marks[:1, :], (height, BLOCK))
        for r in range(row_blocks):
            picked = jnp.where(mark == r, values[:, r * BLOCK : (r + 1) * BLOCK], picked)
        return picked.astype(jnp.bfloat16)

    def product(left, right):
        return jnp.dot(left, right, preferred_element_type=jnp.float32)

    def depart(step, current):
        exact = current * inv_sqrt_degree
        scaled = exact.astype(jnp.bfloat16)
        wide = scaled.astype(jnp.float32)
        if step > 0:
            wide = jnp.concatenate([wide, exact - wide], axis=0)
            scaled = wide.astype(jnp.bfloat16)
        height = wide.shape[0]
        rows = pl.ds(0, height)
        scaled_buf[step, :height] = scaled
        for slot in range(CROSS):
            span = slice(slot * BLOCK, (slot + 1) * BLOCK)
            ahead_out[step, :height, span] = chosen(wide, aim_ref[slot, 1])
        if step == 0:
            pl.semaphore_wait(barrier, len(greeted))
            weights_copy = send(turned_ref, turned_in, edge_send.at[6], edge_recv.at[6], ahead)
            aim_copy = send(aim_ref, aim_in, edge_send.at[7], edge_recv.at[7], ahead)
        ahead_copy = send(
            ahead_out.at[step, rows], behind_in.at[step, rows],
            edge_send.at[2 * step], edge_recv.at[2 * step], ahead,
        )
        pair_copy = send(
            scaled_buf.at[step, rows], partner_buf.at[step, rows],
            pair_send.at[step], pair_recv.at[step], partner,
        )
        if step == 0:
            for r in range(row_blocks):
                span = slice(r * BLOCK, (r + 1) * BLOCK)
                exact = dense_ref[span, :]
                high = exact.astype(jnp.bfloat16)
                high_ref[span, :] = high
                low_ref[span, :] = (exact - high.astype(jnp.float32)).astype(jnp.bfloat16)
                index = lax.broadcasted_iota(jnp.int32, (BLOCK, nodes), 0) + r * BLOCK
                pair_ref[span, :] = (index == partner_ref[...]).astype(jnp.float32).astype(jnp.bfloat16)
            aim_copy.wait_recv()
        for slot in range(CROSS):
            span = slice(slot * BLOCK, (slot + 1) * BLOCK)
            behind_out[step, :height, span] = chosen(wide, aim_in[slot, 0])
        behind_copy = send(
            behind_out.at[step, rows], ahead_in.at[step, rows],
            edge_send.at[2 * step + 1], edge_recv.at[2 * step + 1], behind,
        )
        if step == 0:
            weights_copy.wait_recv()
            for slot in range(CROSS):
                span = slice(slot * BLOCK, (slot + 1) * BLOCK)
                weight = turned_in[span, :].astype(jnp.float32)
                mark = jnp.broadcast_to(aim_in[slot, 0][:1, :], (BLOCK, BLOCK))
                for r in range(row_blocks):
                    forward_weights[span, r * BLOCK : (r + 1) * BLOCK] = jnp.where(
                        mark == r, weight, 0.0
                    ).astype(jnp.bfloat16)
        return height, scaled, pair_copy, ahead_copy, behind_copy

    def nearby(trip):
        return product(trip[1], high_ref[...]) + product(trip[1], low_ref[...])

    def arrive(step, current, trip, total):
        height, _, pair_copy, ahead_copy, behind_copy = trip
        pair_copy.wait_recv()
        total += product(partner_buf[step, :height], pair_ref[...])
        ahead_copy.wait_recv()
        total += product(behind_in[step, :height], forward_weights[...])
        behind_copy.wait_recv()
        total += product(ahead_in[step, :height], back_ref[...])
        if height > vectors:
            total = total[:vectors] + total[vectors:]
        return current + inv_sqrt_degree * total

    bases = [sum(size for _, size in stages[:level]) for level in range(len(stages))]

    def share(which, level, value):
        (stride, size), buf, base = stages[level], gather_bufs[level], bases[level]
        digit = (me // stride) % size
        buf[which, digit] = value
        for shift in range(1, size):
            send(
                buf.at[which, digit], buf.at[which, digit],
                gather_send.at[which, base + shift], gather_recv.at[which, base + digit],
                peer(stride, size, shift)[1],
            )

    def collect(which, level):
        (stride, size), buf, base = stages[level], gather_bufs[level], bases[level]
        digit = (me // stride) % size
        for shift in range(1, size):
            other, device = peer(stride, size, shift)
            pltpu.make_async_remote_copy(
                src_ref=buf.at[which, digit], dst_ref=buf.at[which, other],
                send_sem=gather_send.at[which, base + shift],
                recv_sem=gather_recv.at[which, base + other],
                device_id=device, device_id_type=MESH,
            ).wait_recv()
        value = buf[which, 0]
        for other in range(1, size):
            value = value + buf[which, other]
        return value

    def advance(which, level):
        value = collect(which, level)
        if level + 1 < len(stages):
            share(which, level + 1, value)
        return value

    def folded(value):
        half = vectors // 2
        return jnp.concatenate([value[:half], value[half:]], axis=1)

    def unfolded(value):
        return jnp.concatenate([value[:, :vectors], value[:, vectors:]], axis=0) / node_total

    def inner(left, right):
        return lax.dot_general(
            left, right, (((1,), (1,)), ((), ())), precision=FULL, preferred_element_type=jnp.float32
        )

    def full(left, right):
        return jnp.dot(left, right, precision=FULL, preferred_element_type=jnp.float32)

    last = len(stages) - 1
    start = start_ref[...]
    trip = depart(0, start)
    first = arrive(0, start, trip, nearby(trip))
    trip = depart(1, first)
    share(0, 0, folded(inner(first, first)))
    total = nearby(trip)
    second = arrive(1, first, trip, total)
    trip = depart(2, second)
    advance(0, 0)
    share(1, 0, folded(inner(second, second)))
    total = nearby(trip)
    third = arrive(2, second, trip, total)
    share(2, 0, folded(inner(second, third)))
    for level in range(1, last):
        advance(0, level)
    advance(1, 0)
    first_inverse = inverse_factor(unfolded(collect(0, last)))
    for level in range(last):
        advance(2, level)
        if level + 1 < last:
            advance(1, level + 1)
    middle = inner(full(first_inverse, unfolded(collect(1, last))), first_inverse)
    change = full(inverse_factor(middle), first_inverse)
    subspace_ref[...] = full(change, second)
    rayleigh_ref[...] = inner(full(change, unfolded(collect(2, last))), change)
    for copy in sent:
        copy.wait_send()


def solution(mesh):
    blk_total, scale_total = mesh.shape["blk"], mesh.shape["scale"]
    stages = group_stages(blk_total * scale_total)

    def shards(start_block, blocks, block_column, block_target, block_count, partner, degree):
        vectors, nodes = start_block.shape
        vmem = pl.BlockSpec(memory_space=pltpu.VMEM)
        smem = pl.BlockSpec(memory_space=pltpu.SMEM)
        half = jnp.bfloat16
        hbm = pl.BlockSpec(memory_space=pltpu.HBM)
        slots = block_column.shape[0]
        prepared = pl.pallas_call(
            prepare,
            out_shape=(
                jax.ShapeDtypeStruct((nodes, nodes), jnp.float32),
                jax.ShapeDtypeStruct((CROSS * BLOCK, nodes), half),
                jax.ShapeDtypeStruct((CROSS * BLOCK, BLOCK), half),
                jax.ShapeDtypeStruct((CROSS, 2, 8, BLOCK), jnp.int32),
                jax.ShapeDtypeStruct((1, nodes), jnp.int32),
                jax.ShapeDtypeStruct((vectors, nodes), jnp.float32),
                jax.ShapeDtypeStruct((1, nodes), jnp.float32),
            ),
            in_specs=[smem] + [hbm] * 6,
            out_specs=(vmem,) * 7,
            scratch_shapes=[
                pltpu.SMEM((slots,), jnp.int32),
                pltpu.SMEM((slots,), jnp.int32),
                pltpu.VMEM(blocks.shape, half),
                pltpu.VMEM((1, nodes), jnp.int32),
                pltpu.SemaphoreType.DMA((6,)),
            ],
            compiler_params=pltpu.CompilerParams(vmem_limit_bytes=32 * 2**20),
        )(
            block_count,
            *(
                pltpu.with_memory_space_constraint(array, pltpu.HBM)
                for array in (
                    block_column, block_target, blocks,
                    partner.reshape(1, nodes), start_block, degree.reshape(1, nodes),
                )
            ),
        )
        steps = STEPS
        edge = pltpu.VMEM((steps, 2 * vectors, CROSS * BLOCK), half)
        counts = sum(size for _, size in stages)
        return pl.pallas_call(
            functools.partial(iterate, blk_total, scale_total),
            out_shape=(
                jax.ShapeDtypeStruct((vectors, nodes), jnp.float32),
                jax.ShapeDtypeStruct((vectors, vectors), jnp.float32),
            ),
            in_specs=[vmem] * 7,
            out_specs=(vmem, vmem),
            scratch_shapes=[
                pltpu.VMEM((steps, 2 * vectors, nodes), half),
                pltpu.VMEM((steps, 2 * vectors, nodes), half),
                edge, edge, edge, edge,
                pltpu.VMEM((CROSS * BLOCK, BLOCK), half),
                pltpu.VMEM((CROSS, 2, 8, BLOCK), jnp.int32),
                pltpu.VMEM((CROSS * BLOCK, nodes), half),
                pltpu.VMEM((nodes, nodes), half),
                pltpu.VMEM((nodes, nodes), half),
                pltpu.VMEM((nodes, nodes), half),
                *[
                    pltpu.VMEM((steps, size, vectors // 2, 2 * vectors), jnp.float32)
                    for _, size in stages
                ],
                pltpu.SemaphoreType.DMA((steps,)),
                pltpu.SemaphoreType.DMA((steps,)),
                pltpu.SemaphoreType.DMA((2 * steps + 2,)),
                pltpu.SemaphoreType.DMA((2 * steps + 2,)),
                pltpu.SemaphoreType.DMA((steps, counts)),
                pltpu.SemaphoreType.DMA((steps, counts)),
            ],
            compiler_params=pltpu.CompilerParams(
                collective_id=0, has_side_effects=True, vmem_limit_bytes=40 * 2**20
            ),
        )(*prepared)

    return jax.shard_map(
        shards,
        mesh=mesh,
        in_specs=(
            P(None, ("blk", "scale")),
            P(("blk", "scale"), None, None),
            P(("blk", "scale")),
            P(("blk", "scale")),
            P(("blk", "scale")),
            P(("blk", "scale")),
            P(("blk", "scale")),
        ),
        out_specs=(P(None, ("blk", "scale")), P()),
        check_vma=False,
    )
```
